32 devices in a mesh: pair: 32 (over z, y, x, core), aux: 1.
Axes of the slice: x: 2, y: 2, z: 4, core: 2. Of those that a mesh axis runs over, the one named last changes fastest.
Arguments:
- amplitudes: bfloat16 [32, 256, 256], P('pair'), may hold values from -6 to 6
- ranks: int32 [32], P('pair'), may hold values from 64 to 256
- neighbours: int32 [32, 16], P('pair', 'aux'), may hold values from 0 to 31, as said below
- intersections: bfloat16 [32, 16, 256, 256], P('pair', 'aux'), may hold values from -0.375 to 0.375
- couplings: float32 [32, 16], P('pair', 'aux'), may hold values from -1 to 1
- energies: float32 [32, 256], P('pair'), may hold values from 0.5 to 4
- factors: bfloat16 [32, 2, 5120, 256], P('pair', None, 'aux'), may hold values from -1.75 to 1.75
Outputs:
- residual: float32 [32, 256, 256], P('pair', 'aux')
- updated: float32 [32, 256, 256], P('pair', 'aux')
The draws below stay inside these ranges and needn't reach their ends.
Inputs may be any that keep to these rules, and one draw needn't show every extreme that they name: `neighbours`: the 16 coupled pairs of pair p are distinct and lie among the pairs p - 8 to p + 8, counted modulo 32.
All inputs are finite; a program needn't handle non-finite values.
Results may differ from the reference program's by a relative error of at most 0.0022.
Values may be sent and summed in bfloat16 or wider, within the bound.
No kernel may reach another device: no remote copies, remote signals or barrier semaphores. Data moves between devices by JAX's collectives and lax.ppermute only.
A program may use at most 64 MiB of HBM per device.

```python
import math
import jax
import jax.numpy as jnp
from jax import lax

R = 256
NAUX = 5120
NBR = 16
WIN = 8
PAIRS = 32


def draw_neighbours(key, part):
    keys = jax.random.split(key, PAIRS)
    offsets = jnp.arange(2 * WIN + 1, dtype=jnp.int32) - WIN

    def one_row(row_key):
        return jax.random.permutation(row_key, offsets)[:NBR]
    picked = jax.vmap(one_row)(keys)
    anchor = jnp.arange(PAIRS, dtype=jnp.int32)
    return ((anchor[:, None] + picked) % PAIRS).astype(jnp.int32)


def touch_ends(array, rng, least, high):
    spot = [jax.random.randint(jax.random.fold_in(rng, axis), (), 0, length) for axis, length in enumerate(array.shape)]
    longest = array.shape.index(max(array.shape))
    next_to = spot[:longest] + [(spot[longest] + 1) % array.shape[longest]] + spot[longest + 1:]
    return array.at[tuple(spot)].set(least).at[tuple(next_to)].set(high)


def steps_of(own_key, dims, shards, smallest, high):
    level, own = 1.0, jax.random.fold_in(own_key, 6)
    for axis_at, blocks in shards:
        heights = jnp.exp(jax.random.uniform(jax.random.fold_in(own, axis_at), (blocks,), jnp.float32, smallest / len(shards), high / len(shards)))
        level = level * jnp.repeat(heights, dims[axis_at] // blocks).reshape([-1 if axis == axis_at else 1 for axis in range(len(dims))])
    return level


def gaussian(key, dims, spread, most, cuts=(), held_as=jnp.bfloat16):
    array = spread * jax.random.normal(key, dims, jnp.float32)
    if cuts:
        array = array * steps_of(key, dims, cuts, -0.22, 0.18)
    return jnp.clip(array, -most, most).astype(held_as)


def setup_inputs(seed: int = 0) -> dict:
    seeds = jax.random.split(jax.random.key(seed), 8)
    amplitudes = gaussian(seeds[0], (PAIRS, R, R), 1.0, 6.0, ((0, 32),))
    ranks = touch_ends(jax.random.randint(seeds[1], (PAIRS,), R // 4, R + 1), jax.random.fold_in(seeds[1], 1), R // 4, R).astype(jnp.int32)
    neighbours = draw_neighbours(jax.random.fold_in(seeds[7], 71), 0)
    intersections = gaussian(seeds[3], (PAIRS, NBR, R, R), R ** -0.5, 0.375, ((0, 32),))
    couplings = jnp.clip(jax.random.uniform(seeds[4], (PAIRS, NBR), jnp.float32, -1.0, 1.0) * steps_of(seeds[4], (PAIRS, NBR), ((0, 32),), -0.4, 0.0), -1.0, 1.0)
    energies = jnp.clip(jnp.exp(math.log(4.0) - 2.0794415 * jax.random.uniform(seeds[5], (PAIRS, R), jnp.float32) ** steps_of(seeds[5], (PAIRS, R), ((0, 32),), -0.2, 0.2)), 0.5, 4.0)
    factors = gaussian(seeds[6], (PAIRS, 2, NAUX, R), (NAUX ** -0.25), 1.75, ((0, 32),))
    return {"amplitudes": amplitudes, "ranks": ranks, "neighbours": neighbours, "intersections": intersections, "couplings": couplings, "energies": energies, "factors": factors}


def reference(amplitudes, ranks, neighbours, intersections, couplings, energies, factors):
    positions = jnp.arange(R)
    live_rows = positions[None, :] < ranks[:, None]
    square_mask = live_rows[:, :, None] & live_rows[:, None, :]
    masked = jnp.where(square_mask, amplitudes, jnp.zeros((), amplitudes.dtype))

    def one_pair(index):
        pair_factors = factors[index]
        partial_sum = jnp.dot(pair_factors[0].T, pair_factors[1], preferred_element_type=jnp.float32)
        for column in range(NBR):
            picked = masked[neighbours[index, column]]
            intersection_now = intersections[index, column]
            half_product = jnp.dot(intersection_now, picked, preferred_element_type=jnp.float32).astype(jnp.bfloat16)
            projected = jnp.dot(half_product, intersection_now.T, preferred_element_type=jnp.float32)
            partial_sum = partial_sum + couplings[index, column] * projected
        energy_row = energies[index]
        denominator = energy_row[:, None] + energy_row[None, :]
        own_amp = masked[index].astype(jnp.float32)
        residual = jnp.where(square_mask[index], partial_sum + denominator * own_amp, jnp.zeros((), jnp.float32))
        return residual, own_amp - residual / denominator

    residual, updated = lax.map(one_pair, jnp.arange(PAIRS))
    return residual, updated
```

```python
import functools

import jax
import jax.numpy as jnp
from jax import lax
from jax.experimental import pallas as pl
from jax.experimental.pallas import tpu as pltpu
from jax.sharding import PartitionSpec as P

WIN = 8
F32 = jnp.float32


def permuted(value, axis, target):
    count = lax.axis_size(axis)
    return lax.ppermute(value, axis, [(source, target(source)) for source in range(count)])


def swapped(value, axis, bits):
    return permuted(value, axis, lambda source: source ^ bits)


def shifted(value, axis, steps):
    count = lax.axis_size(axis)
    return permuted(value, axis, lambda source: (source + steps) % count)


def top_bit(number):
    return 1 << (number.bit_length() - 1)


def gathered(masked, axis):
    count = lax.axis_size(axis)
    me = lax.axis_index(axis)
    before = shifted(masked, axis, WIN)
    after = shifted(masked, axis, -WIN)
    own = {0: masked}
    for bits in range(2, WIN, 2):
        own[bits] = swapped(masked, axis, bits)
    before, after, own = lax.optimization_barrier((before, after, own))

    def side(bits):
        return jnp.where((me & top_bit(bits)) != 0, before, after)

    far = {bits: swapped(side(bits), axis, bits) for bits in range(2, WIN, 2)}
    for bits in range(1, WIN, 2):
        own[bits] = swapped(own[bits - 1], axis, 1)
    far[1] = swapped(side(1), axis, 1)
    for bits in range(3, WIN, 2):
        far[bits] = swapped(far[bits - 1], axis, 1)
    blocks = [(me ^ bits, own[bits]) for bits in range(WIN)]
    for bits in range(1, WIN):
        other = me ^ bits
        blocks.append((jnp.where(other > me, other - WIN, other + WIN), far[bits]))
    blocks.append((me - WIN, before))
    blocks.append((me + WIN, after))
    return [((source + count) % count, block) for source, block in blocks]


def coupled_kernel(count, slots, sources, neighbours, couplings, *refs):
    blocks, (inter, start, total) = refs[:count], refs[count:]
    sum_now = start[...]
    for position in range(count):
        slot, factor = jnp.int32(0), jnp.float32(0)
        for n in range(slots):
            hit = neighbours[0, n] == sources[position]
            slot = jnp.where(hit, n, slot)
            factor = jnp.where(hit, couplings[0, n], factor)
        inter_now = inter[slot]
        half = jnp.dot(inter_now, blocks[position][...], preferred_element_type=F32).astype(jnp.bfloat16)
        projected = lax.dot_general(
            half, inter_now, (((1,), (1,)), ((), ())), preferred_element_type=F32
        )
        sum_now = sum_now + factor * projected
    total[...] = sum_now


def coupled(blocks, neighbours, couplings, intersections, start):
    count, slots = len(blocks), neighbours.shape[1]
    sources = jnp.stack([source for source, _ in blocks]).astype(jnp.int32)
    arrays = [block[0] for _, block in blocks]
    vmem = pl.BlockSpec(memory_space=pltpu.VMEM)
    smem = pl.BlockSpec(memory_space=pltpu.SMEM)
    width = start.shape[0]
    return pl.pallas_call(
        functools.partial(coupled_kernel, count, slots),
        out_shape=jax.ShapeDtypeStruct(start.shape, F32),
        in_specs=[smem] * 3 + [vmem] * (count + 2),
        out_specs=vmem,
        compiler_params=pltpu.CompilerParams(vmem_limit_bytes=24 << 20),
        cost_estimate=pl.CostEstimate(
            flops=4 * count * width**3, bytes_accessed=2 * (slots + count) * width**2, transcendentals=0
        ),
    )(sources, neighbours, couplings, *arrays, intersections[0], start)


def shards(amplitudes, ranks, neighbours, intersections, couplings, energies, factors):
    pno_width = amplitudes.shape[1]
    aux_count = lax.axis_size("aux")
    row_span = pno_width // aux_count
    first_row = lax.axis_index("aux") * row_span
    positions = jnp.arange(pno_width)
    live_rows = positions[None, :] < ranks[:, None]
    square_mask = live_rows[:, :, None] & live_rows[:, None, :]
    masked = jnp.where(square_mask, amplitudes, jnp.zeros((), jnp.bfloat16))
    blocks = gathered(masked, "pair")
    exchange = jnp.einsum("qa,qb->ab", factors[0, 0], factors[0, 1], preferred_element_type=F32)
    partial_sum = coupled(blocks, neighbours, couplings, intersections, exchange)[None]
    summed = lax.psum_scatter(partial_sum, "aux", scatter_dimension=1, tiled=True)
    row_energy = lax.dynamic_slice_in_dim(energies, first_row, row_span, 1)
    denominator = row_energy[:, :, None] + energies[:, None, :]
    row_amp = lax.dynamic_slice_in_dim(masked, first_row, row_span, 1).astype(F32)
    row_mask = lax.dynamic_slice_in_dim(square_mask, first_row, row_span, 1)
    residual = jnp.where(row_mask, summed + denominator * row_amp, jnp.zeros((), F32))
    return (residual, row_amp - residual / denominator)


def solution(mesh):
    return jax.shard_map(
        shards,
        mesh=mesh,
        in_specs=(
            P("pair", None, None),
            P("pair"),
            P("pair", "aux"),
            P("pair", "aux", None, None),
            P("pair", "aux"),
            P("pair", None),
            P("pair", None, "aux", None),
        ),
        out_specs=(P("pair", "aux", None), P("pair", "aux", None)),
        check_vma=False,
    )
```

```python
import functools

import jax
import jax.numpy as jnp
from jax import lax
from jax.experimental import pallas as pl
from jax.experimental.pallas import tpu as pltpu
from jax.sharding import PartitionSpec as P

WIN = 8
F32 = jnp.float32
BF16 = jnp.bfloat16
VMEM = pl.BlockSpec(memory_space=pltpu.VMEM)
SMEM = pl.BlockSpec(memory_space=pltpu.SMEM)


def permuted(value, axis, target):
    count = lax.axis_size(axis)
    return lax.ppermute(value, axis, [(source, target(source)) for source in range(count)])


def swapped(value, axis, bits):
    return permuted(value, axis, lambda source: source ^ bits)


def shifted(value, axis, steps):
    count = lax.axis_size(axis)
    return permuted(value, axis, lambda source: (source + steps) % count)


def top_bit(number):
    return 1 << (number.bit_length() - 1)


def held(*arrays):
    return [pltpu.with_memory_space_constraint(array, pltpu.VMEM) for array in arrays]


def live_square(rank, shape):
    rows = lax.broadcasted_iota(jnp.int32, shape, 0)
    columns = lax.broadcasted_iota(jnp.int32, shape, 1)
    return jnp.maximum(rows, columns) < rank


def mask_kernel(rank, amplitude, masked):
    square = live_square(rank[0], amplitude.shape)
    masked[...] = jnp.where(square, amplitude[...].astype(F32), 0.0).astype(BF16)


def mask(ranks, amplitude):
    return pl.pallas_call(
        mask_kernel,
        out_shape=jax.ShapeDtypeStruct(amplitude.shape, BF16),
        in_specs=[SMEM, VMEM],
        out_specs=VMEM,
    )(ranks, amplitude)


def coupled_sum(sources, neighbours, couplings, inter, blocks, sum_now):
    for position, block in enumerate(blocks):
        slot, factor = jnp.int32(0), jnp.float32(0)
        for n in range(neighbours.shape[1]):
            hit = neighbours[0, n] == sources[position]
            slot = jnp.where(hit, n, slot)
            factor = jnp.where(hit, couplings[0, n], factor)
        inter_now = inter[slot]
        half = jnp.dot(inter_now, block[...], preferred_element_type=F32).astype(BF16)
        projected = lax.dot_general(
            half, inter_now, (((1,), (1,)), ((), ())), preferred_element_type=F32
        )
        sum_now = sum_now + factor * projected
    return sum_now


def coupled_kernel(count, sources, neighbours, couplings, *refs):
    blocks, (inter, start, total) = refs[:count], refs[count:]
    total[...] = coupled_sum(sources, neighbours, couplings, inter, blocks, start[...])


def last_kernel(count, sources, neighbours, couplings, *refs):
    blocks, (inter, start, rank, energy, masked, residual, updated) = refs[:count], refs[count:]
    total = coupled_sum(sources, neighbours, couplings, inter, blocks, start[...])
    along = jnp.broadcast_to(energy[...], total.shape)
    denominator = along + along.T
    own = masked[...].astype(F32)
    square = live_square(rank[0], total.shape)
    residual_now = jnp.where(square, total + denominator * own, 0.0)
    residual[...] = residual_now
    updated[...] = own - residual_now / denominator


def coupled(blocks, neighbours, couplings, inter, start, ending=None):
    count, slots, width = len(blocks), neighbours.shape[1], start.shape[0]
    sources = jnp.stack([source for source, _ in blocks]).astype(jnp.int32)
    arrays = held(*[block for _, block in blocks], inter, start)
    shape = jax.ShapeDtypeStruct(start.shape, F32)
    cost = pl.CostEstimate(
        flops=4 * count * width**3, bytes_accessed=2 * (slots + count) * width**2, transcendentals=0
    )
    params = pltpu.CompilerParams(vmem_limit_bytes=4 << 20)
    in_specs = [SMEM] * 3 + [VMEM] * (count + 2)
    if ending is None:
        return pl.pallas_call(
            functools.partial(coupled_kernel, count),
            out_shape=shape,
            in_specs=in_specs,
            out_specs=VMEM,
            compiler_params=params,
            cost_estimate=cost,
        )(sources, neighbours, couplings, *arrays)
    ranks, energies, masked = ending
    return pl.pallas_call(
        functools.partial(last_kernel, count),
        out_shape=(shape, shape),
        in_specs=in_specs + [SMEM, VMEM, VMEM],
        out_specs=(VMEM, VMEM),
        compiler_params=params,
        cost_estimate=cost,
    )(sources, neighbours, couplings, *arrays, ranks, energies, *held(masked))


def shards(amplitudes, ranks, neighbours, intersections, couplings, energies, factors):
    pno_width = amplitudes.shape[1]
    aux_count = lax.axis_size("aux")
    axis = "pair"
    count = lax.axis_size(axis)
    me = lax.axis_index(axis)
    masked = mask(ranks, amplitudes[0])
    inter = intersections[0]

    own = {0: masked}
    for bits in reversed(range(2, WIN, 2)):
        own[bits] = swapped(masked, axis, bits)
    after = shifted(masked, axis, -WIN)
    before = shifted(masked, axis, WIN)
    own[2], own[4], after, before = lax.optimization_barrier((own[2], own[4], after, before))

    def side(bits):
        return jnp.where((me & top_bit(bits)) != 0, before, after)

    far = {bits: swapped(side(bits), axis, bits) for bits in range(2, WIN, 2)}
    for bits in range(1, WIN, 2):
        own[bits] = swapped(own[bits - 1], axis, 1)
    far[1] = swapped(side(1), axis, 1)
    own[3], factors = lax.optimization_barrier((own[3], factors))
    exchange = jnp.einsum("qa,qb->ab", factors[0, 0], factors[0, 1], preferred_element_type=F32)
    near_blocks = [(me ^ bits, own[bits]) for bits in range(WIN)]
    partial_sum = coupled(near_blocks, neighbours, couplings, inter, exchange)
    far, partial_sum = lax.optimization_barrier((far, partial_sum))

    def far_source(bits):
        other = me ^ bits
        return jnp.where(other > me, other - WIN + count, other + WIN) % count

    for bits in range(3, WIN, 2):
        far[bits] = swapped(far[bits - 1], axis, 1)
    far_blocks = [((me - WIN + count) % count, before), ((me + WIN) % count, after)]
    far_blocks += [(far_source(bits), far[bits]) for bits in (1, *range(2, WIN, 2))]
    partial_sum = coupled(far_blocks, neighbours, couplings, inter, partial_sum)
    far_blocks = [(far_source(bits), far[bits]) for bits in range(3, WIN, 2)]
    if aux_count == 1:
        residual, updated = coupled(
            far_blocks, neighbours, couplings, inter, partial_sum, (ranks, energies, masked)
        )
        return residual[None], updated[None]

    partial_sum = coupled(far_blocks, neighbours, couplings, inter, partial_sum)[None]
    row_span = pno_width // aux_count
    first_row = lax.axis_index("aux") * row_span
    live_rows = jnp.arange(pno_width)[None, :] < ranks[:, None]
    square_mask = live_rows[:, :, None] & live_rows[:, None, :]
    summed = lax.psum_scatter(partial_sum, "aux", scatter_dimension=1, tiled=True)
    row_energy = lax.dynamic_slice_in_dim(energies, first_row, row_span, 1)
    denominator = row_energy[:, :, None] + energies[:, None, :]
    row_amp = lax.dynamic_slice_in_dim(masked[None], first_row, row_span, 1).astype(F32)
    row_mask = lax.dynamic_slice_in_dim(square_mask, first_row, row_span, 1)
    residual = jnp.where(row_mask, summed + denominator * row_amp, jnp.zeros((), F32))
    return (residual, row_amp - residual / denominator)


def solution(mesh):
    return jax.shard_map(
        shards,
        mesh=mesh,
        in_specs=(
            P("pair", None, None),
            P("pair"),
            P("pair", "aux"),
            P("pair", "aux", None, None),
            P("pair", "aux"),
            P("pair", None),
            P("pair", None, "aux", None),
        ),
        out_specs=(P("pair", "aux", None), P("pair", "aux", None)),
        check_vma=False,
    )
```

```python
import functools

import jax
import jax.numpy as jnp
from jax import lax
from jax.experimental import pallas as pl
from jax.experimental.pallas import tpu as pltpu
from jax.sharding import PartitionSpec as P

WIN = 8
F32 = jnp.float32
BF16 = jnp.bfloat16
VMEM = pl.BlockSpec(memory_space=pltpu.VMEM)
SMEM = pl.BlockSpec(memory_space=pltpu.SMEM)
PARAMS = pltpu.CompilerParams(vmem_limit_bytes=4 << 20)


def permuted(value, axis, target):
    count = lax.axis_size(axis)
    return lax.ppermute(value, axis, [(source, target(source)) for source in range(count)])


def swapped(value, axis, bits):
    return permuted(value, axis, lambda source: source ^ bits)


def shifted(value, axis, steps):
    count = lax.axis_size(axis)
    return permuted(value, axis, lambda source: (source + steps) % count)


def top_bit(number):
    return 1 << (number.bit_length() - 1)


def held(*arrays):
    return [pltpu.with_memory_space_constraint(array, pltpu.VMEM) for array in arrays]


def live_square(rank, shape):
    rows = lax.broadcasted_iota(jnp.int32, shape, 0)
    columns = lax.broadcasted_iota(jnp.int32, shape, 1)
    return jnp.maximum(rows, columns) < rank


def cost(count, width):
    return pl.CostEstimate(
        flops=4 * count * width**3, bytes_accessed=4 * count * width**2, transcendentals=0
    )


def mask_kernel(rank, amplitude, masked):
    square = live_square(rank[...], amplitude.shape)
    masked[...] = jnp.where(square, amplitude[...].astype(F32), 0.0).astype(BF16)


def mask(ranks, amplitude):
    return pl.pallas_call(
        mask_kernel,
        out_shape=pltpu.VMEM(amplitude.shape, BF16),
        in_specs=[VMEM, VMEM],
        out_specs=VMEM,
    )(ranks[None], amplitude)


def pack_kernel(axis, *refs):
    (before, after), own = refs[:2], refs[2 : 2 + WIN // 2]
    packed, *sides = refs[2 + WIN // 2 :]
    me = lax.axis_index(axis)
    for position, block in enumerate(own):
        packed[position] = block[...]
    for bits, side in zip((1, 2, 4), (packed.at[len(own)], *sides)):
        side[...] = jnp.where((me & bits) != 0, before[...], after[...])


def pack(axis, before, after, own):
    shape = pltpu.VMEM(before.shape, BF16)
    arrays = held(before, after, *own)
    return pl.pallas_call(
        functools.partial(pack_kernel, axis),
        out_shape=(pltpu.VMEM((len(own) + 1, *before.shape), BF16), shape, shape),
        in_specs=[VMEM] * len(arrays),
        out_specs=(VMEM,) * 3,
        compiler_params=PARAMS,
    )(*arrays)


def one_term(inter, block, factor):
    half = jnp.dot(inter, block, preferred_element_type=F32).astype(BF16)
    projected = lax.dot_general(
        half, inter, (((1,), (1,)), ((), ())), preferred_element_type=F32
    )
    return factor * projected


def find(position, sources, neighbours, couplings):
    slot, factor = jnp.int32(0), jnp.float32(0)
    for n in range(neighbours.shape[1]):
        hit = neighbours[0, n] == sources[position]
        slot = jnp.where(hit, n, slot)
        factor = jnp.where(hit, couplings[0, n], factor)
    return slot, factor


def near_kernel(
    whole, sources, neighbours, couplings, rank, energy, inter, start, mine, theirs,
    total, scale, far_inter, far_factor, near_inter, sems,
):
    near = [ref.at[k] for ref in (mine, theirs) for k in range(WIN // 2)]
    copies, factors = [], []
    for position in range(sources.shape[0]):
        slot, factor = find(position, sources, neighbours, couplings)
        far = position - len(near)
        target = near_inter.at[position] if far < 0 else far_inter.at[far]
        copy = pltpu.make_async_copy(inter.at[slot], target, sems.at[position])
        copy.start()
        copies.append(copy)
        factors.append(factor)
    along = jnp.broadcast_to(energy[...], total.shape)
    denominator = along + along.T
    sum_now = start[...]
    if whole:
        sum_now = sum_now + denominator * mine[0].astype(F32)
    scale[...] = jnp.where(live_square(rank[...], total.shape), 1.0 / denominator, 0.0)
    for far in range(far_inter.shape[0]):
        far_factor[far] = jnp.full(far_factor.shape[1:], factors[len(near) + far], F32)
    for position, block in enumerate(near):
        copies[position].wait()
        sum_now = sum_now + one_term(near_inter[position], block[...], factors[position])
    total[...] = sum_now
    for copy in copies[len(near):]:
        copy.wait()


def near_sum(whole, sources, neighbours, couplings, ranks, energies, inter, start, mine, theirs):
    far = sources.shape[0] - WIN
    width = start.shape[0]
    inter = pltpu.with_memory_space_constraint(inter, pltpu.HBM)
    return pl.pallas_call(
        functools.partial(near_kernel, whole),
        out_shape=(
            pltpu.VMEM(start.shape, F32),
            pltpu.VMEM(start.shape, F32),
            pltpu.VMEM((far, width, width), BF16),
            pltpu.VMEM((far, 1, width), F32),
        ),
        in_specs=[SMEM] * 3 + [VMEM] * 2 + [pl.BlockSpec(memory_space=pl.ANY)] + [VMEM] * 3,
        out_specs=(VMEM,) * 4,
        scratch_shapes=[
            pltpu.VMEM((WIN, width, width), BF16),
            pltpu.SemaphoreType.DMA((sources.shape[0],)),
        ],
        compiler_params=PARAMS,
        cost_estimate=cost(WIN, width),
    )(sources, neighbours, couplings, ranks[None], energies, inter, *held(start, mine, theirs))


def far_kernel(first, count, far_inter, far_factor, start, *refs):
    sum_now = start[...]
    for position in range(count):
        block = refs[position]
        block = block[...] if len(block.shape) == 2 else block[block.shape[0] - 1]
        sum_now = sum_now + one_term(
            far_inter[first + position], block, far_factor[first + position]
        )
    if len(refs) == count + 1:
        refs[count][...] = sum_now
    else:
        scale, masked, residual, updated = refs[count:]
        residual[...] = jnp.where(scale[...] > 0, sum_now, 0.0)
        updated[...] = masked[...].astype(F32) - sum_now * scale[...]


def far_sum(first, far_inter, far_factor, start, blocks, ending=()):
    out_shape = pltpu.VMEM(start.shape, F32)
    if ending:
        out_shape = (jax.ShapeDtypeStruct(start.shape, F32),) * 2
    arrays = held(far_inter, far_factor, start, *blocks, *ending)
    return pl.pallas_call(
        functools.partial(far_kernel, first, len(blocks)),
        out_shape=out_shape,
        in_specs=[VMEM] * len(arrays),
        out_specs=(VMEM, VMEM) if ending else VMEM,
        compiler_params=PARAMS,
        cost_estimate=cost(len(blocks), start.shape[0]),
    )(*arrays)


def shards(amplitudes, ranks, neighbours, intersections, couplings, energies, factors):
    aux_count = lax.axis_size("aux")
    axis = "pair"
    count = lax.axis_size(axis)
    me = lax.axis_index(axis)
    masked = mask(ranks, amplitudes[0])
    cross = range(2, WIN, 2)

    own = {0: masked}
    for bits in reversed(cross):
        own[bits] = swapped(masked, axis, bits)
    after = shifted(masked, axis, -WIN)
    before = shifted(masked, axis, WIN)
    exchange = jnp.einsum("qa,qb->ab", factors[0, 0], factors[0, 1], preferred_element_type=F32)
    own[2], own[4], after, before, exchange = lax.optimization_barrier(
        (own[2], own[4], after, before, exchange)
    )
    mine, side2, side4 = pack(axis, before, after, [own[bits] for bits in (0, *cross)])
    far = {2: swapped(side2, axis, 2), 4: swapped(side4, axis, 4)}
    far[6] = permuted(
        own[6], axis, lambda source: (source + (-WIN if source & top_bit(6) else WIN)) % count
    )
    theirs = swapped(mine, axis, 1)

    def far_source(bits):
        other = me ^ bits
        return jnp.where(other > me, other - WIN + count, other + WIN) % count

    sources = [me ^ bits for bits in (*range(0, WIN, 2), *range(1, WIN, 2))]
    sources += [(me - WIN + count) % count, (me + WIN) % count]
    sources += [far_source(bits) for bits in (1, *cross, *range(3, WIN, 2))]
    sources = jnp.stack(sources).astype(jnp.int32)
    total, scale, far_inter, far_factor = near_sum(
        aux_count == 1, sources, neighbours, couplings, ranks, energies, intersections[0], exchange, mine, theirs
    )
    far, total, scale, far_inter, far_factor = lax.optimization_barrier(
        (far, total, scale, far_inter, far_factor)
    )
    early = [before, after, theirs, *(far[bits] for bits in cross)]
    late = [swapped(far[bits], axis, 1) for bits in cross]
    total = far_sum(0, far_inter, far_factor, total, early)
    if aux_count == 1:
        residual, updated = far_sum(len(early), far_inter, far_factor, total, late, (scale, masked))
        return residual[None], updated[None]

    partial_sum = far_sum(len(early), far_inter, far_factor, total, late)[None]
    pno_width = amplitudes.shape[1]
    row_span = pno_width // aux_count
    first_row = lax.axis_index("aux") * row_span
    live_rows = jnp.arange(pno_width)[None, :] < ranks[:, None]
    square_mask = live_rows[:, :, None] & live_rows[:, None, :]
    summed = lax.psum_scatter(partial_sum, "aux", scatter_dimension=1, tiled=True)
    row_energy = lax.dynamic_slice_in_dim(energies, first_row, row_span, 1)
    denominator = row_energy[:, :, None] + energies[:, None, :]
    row_amp = lax.dynamic_slice_in_dim(masked[None], first_row, row_span, 1).astype(F32)
    row_mask = lax.dynamic_slice_in_dim(square_mask, first_row, row_span, 1)
    residual = jnp.where(row_mask, summed + denominator * row_amp, jnp.zeros((), F32))
    return (residual, row_amp - residual / denominator)


def solution(mesh):
    return jax.shard_map(
        shards,
        mesh=mesh,
        in_specs=(
            P("pair", None, None),
            P("pair"),
            P("pair", "aux"),
            P("pair", "aux", None, None),
            P("pair", "aux"),
            P("pair", None),
            P("pair", None, "aux", None),
        ),
        out_specs=(P("pair", "aux", None), P("pair", "aux", None)),
        check_vma=False,
    )
```

```python
import functools

import jax
import jax.numpy as jnp
from jax import lax
from jax.experimental import pallas as pl
from jax.experimental.pallas import tpu as pltpu
from jax.sharding import PartitionSpec as P

WIN = 8
F32 = jnp.float32
BF16 = jnp.bfloat16
VMEM = pl.BlockSpec(memory_space=pltpu.VMEM)
CHUNKS = 5
SMEM = pl.BlockSpec(memory_space=pltpu.SMEM)
ANY = pl.BlockSpec(memory_space=pl.ANY)
PARAMS = pltpu.CompilerParams(vmem_limit_bytes=4 << 20)


def permuted(value, axis, target):
    count = lax.axis_size(axis)
    return lax.ppermute(value, axis, [(source, target(source)) for source in range(count)])


def swapped(value, axis, bits):
    return permuted(value, axis, lambda source: source ^ bits)


def shifted(value, axis, steps):
    count = lax.axis_size(axis)
    return permuted(value, axis, lambda source: (source + steps) % count)


def top_bit(number):
    return 1 << (number.bit_length() - 1)


def held(*arrays):
    return [pltpu.with_memory_space_constraint(array, pltpu.VMEM) for array in arrays]


def live_square(rank, shape):
    rows = lax.broadcasted_iota(jnp.int32, shape, 0)
    columns = lax.broadcasted_iota(jnp.int32, shape, 1)
    return jnp.maximum(rows, columns) < rank


def cost(count, width):
    return pl.CostEstimate(
        flops=4 * count * width**3, bytes_accessed=4 * count * width**2, transcendentals=0
    )


def mask_kernel(rank, amplitude, masked):
    square = live_square(rank[...], amplitude.shape)
    masked[...] = jnp.where(square, amplitude[...].astype(F32), 0.0).astype(BF16)


def mask(ranks, amplitude):
    return pl.pallas_call(
        mask_kernel,
        out_shape=pltpu.VMEM(amplitude.shape, BF16),
        in_specs=[VMEM, VMEM],
        out_specs=VMEM,
    )(ranks[None], amplitude)


def sides_kernel(axis, before, after, *sides):
    me = lax.axis_index(axis)
    for bits, side in zip((1, 2, 4), sides):
        side[...] = jnp.where((me & bits) != 0, before[...], after[...])


def sides_of(axis, before, after):
    return pl.pallas_call(
        functools.partial(sides_kernel, axis),
        out_shape=(pltpu.VMEM(before.shape, BF16),) * 3,
        in_specs=[VMEM] * 2,
        out_specs=(VMEM,) * 3,
        compiler_params=PARAMS,
    )(*held(before, after))


def stack_kernel(*refs):
    for position, block in enumerate(refs[:-1]):
        refs[-1][position] = block[...]


def stacked(*blocks):
    return pl.pallas_call(
        stack_kernel,
        out_shape=pltpu.VMEM((len(blocks), *blocks[0].shape), BF16),
        in_specs=[VMEM] * len(blocks),
        out_specs=VMEM,
        compiler_params=PARAMS,
    )(*held(*blocks))


def one_term(inter, block, factor):
    half = jnp.dot(inter, block, preferred_element_type=F32).astype(BF16)
    projected = lax.dot_general(
        half, inter, (((1,), (1,)), ((), ())), preferred_element_type=F32
    )
    return factor * projected


def stage_kernel(
    whole, axis, places, neighbours, couplings, rank, energy, masked, inter, integrals,
    total, scale, staged, factor, factors, used, held_integrals, sems, integral_sems,
):
    chunks, span = held_integrals.shape[1:3]
    integral_copies = [
        [
            pltpu.make_async_copy(
                integrals.at[side, pl.ds(chunk * span, span)],
                held_integrals.at[side, chunk],
                integral_sems.at[side, chunk],
            )
            for side in range(2)
        ]
        for chunk in range(chunks)
    ]
    for pair in integral_copies:
        for copy in pair:
            copy.start()
    count = lax.axis_size(axis)
    first = WIN - lax.axis_index(axis)
    slots, blocks = neighbours.shape[1], staged.shape[0]
    for position in range(blocks):
        factors[position] = jnp.float32(0)
        used[position] = 0
    copies = []
    for slot in range(slots):
        step = neighbours[0, slot] + first
        step = jnp.where(step < 0, step + count, step)
        position = places[jnp.where(step >= count, step - count, step)]
        factors[position] = couplings[0, slot]
        used[position] = 1
        copies.append(pltpu.make_async_copy(inter.at[slot], staged.at[position], sems.at[slot]))
        copies[-1].start()
    along = jnp.broadcast_to(energy[...], total.shape)
    denominator = along + along.T
    sum_now = jnp.zeros(total.shape, F32)
    if whole:
        sum_now = denominator * masked[...].astype(F32)
    scale[...] = jnp.where(live_square(rank[...], total.shape), 1.0 / denominator, 0.0)
    for position in range(blocks):

        @pl.when(used[position] == 0)
        def _():
            staged[position] = jnp.zeros(staged.shape[1:], BF16)

        factor[position] = jnp.full(factor.shape[1:], factors[position], F32)
    for chunk, pair in enumerate(integral_copies):
        for copy in pair:
            copy.wait()
        sum_now = sum_now + lax.dot_general(
            held_integrals[0, chunk], held_integrals[1, chunk], (((0,), (0,)), ((), ())),
            preferred_element_type=F32,
        )
    total[...] = sum_now
    for copy in copies:
        copy.wait()


def stage(whole, axis, places, neighbours, couplings, ranks, energies, masked, inter, integrals):
    blocks, width = places.shape[0], masked.shape[0]
    square = pltpu.VMEM((width, width), F32)
    energies, neighbours, couplings, inter, integrals = (
        pltpu.with_memory_space_constraint(array, pltpu.HBM)
        for array in (energies, neighbours, couplings, inter, integrals)
    )
    rows = integrals.shape[1]
    chunks = CHUNKS
    return pl.pallas_call(
        functools.partial(stage_kernel, whole, axis),
        out_shape=(
            square,
            square,
            pltpu.VMEM((blocks, width, width), BF16),
            pltpu.VMEM((blocks, 1, width), F32),
        ),
        in_specs=[SMEM] * 3 + [VMEM] * 3 + [ANY] * 2,
        out_specs=(VMEM,) * 4,
        scratch_shapes=[
            pltpu.SMEM((blocks,), F32),
            pltpu.SMEM((blocks,), jnp.int32),
            pltpu.VMEM((2, chunks, rows // chunks, width), BF16),
            pltpu.SemaphoreType.DMA((neighbours.shape[1],)),
            pltpu.SemaphoreType.DMA((2, chunks)),
        ],
        compiler_params=pltpu.CompilerParams(vmem_limit_bytes=9 << 20),
        cost_estimate=cost(WIN, width),
    )(places, neighbours, couplings, ranks[None], energies, *held(masked), inter, integrals)


def sum_kernel(first, picks, starts, inter, factors, *refs):
    sum_now = refs[0][...]
    for ref in refs[1:starts]:
        sum_now = sum_now + ref[...]
    refs = refs[starts:]
    position = first
    for ref, pick in zip(refs, picks):
        for index in pick:
            block = ref[...] if index is None else ref[index]
            sum_now = sum_now + one_term(inter[position], block, factors[position])
            position += 1
    refs = refs[len(picks) :]
    if len(refs) == 1:
        refs[0][...] = sum_now
    else:
        scale, masked, residual, updated = refs
        residual[...] = jnp.where(scale[...] > 0, sum_now, 0.0)
        updated[...] = masked[...].astype(F32) - sum_now * scale[...]


def block_sum(first, inter, factors, starts, blocks, ending=()):
    shape = starts[0].shape
    out_shape = pltpu.VMEM(shape, F32)
    if ending:
        out_shape = (jax.ShapeDtypeStruct(shape, F32),) * 2
    picks = [pick for _, pick in blocks]
    arrays = held(inter, factors, *starts, *(block for block, _ in blocks), *ending)
    return pl.pallas_call(
        functools.partial(sum_kernel, first, picks, len(starts)),
        out_shape=out_shape,
        in_specs=[VMEM] * len(arrays),
        out_specs=(VMEM, VMEM) if ending else VMEM,
        compiler_params=PARAMS,
        cost_estimate=cost(sum(map(len, picks)) * (1 if ending or first else 32), shape[0]),
    )(*arrays)


def shards(amplitudes, ranks, neighbours, intersections, couplings, energies, pair_factors):
    aux_count = lax.axis_size("aux")
    axis = "pair"
    count = lax.axis_size(axis)
    me = lax.axis_index(axis)
    masked = mask(ranks, amplitudes[0])
    cross = range(2, WIN, 2)

    def far_source(bits):
        other = me ^ bits
        return jnp.where(other > me, other - WIN + count, other + WIN) % count

    sources = [me ^ bits for bits in range(0, WIN, 2)]
    sources += [(me - WIN + count) % count, (me + WIN) % count]
    sources += [far_source(bits) for bits in cross]
    sources += [me ^ bits for bits in range(1, WIN, 2)]
    sources += [far_source(bits) for bits in range(1, WIN, 2)]
    steps = [(source - me + WIN + count) % count for source in sources]
    order = jnp.arange(len(sources), dtype=jnp.int32)
    places = jnp.sum(
        jnp.where(jnp.stack(steps)[:, None] == order[None, :], order[:, None], 0), axis=0
    ).astype(jnp.int32)

    own = {0: masked}
    for bits in reversed(cross):
        own[bits] = swapped(masked, axis, bits)
    after = shifted(masked, axis, -WIN)
    before = shifted(masked, axis, WIN)
    staged = stage(
        aux_count == 1, axis, places, neighbours, couplings, ranks, energies, masked, intersections[0], pair_factors[0]
    )
    before, after = lax.optimization_barrier((before, after))
    total, scale, inter, factors = staged
    side1, side2, side4 = sides_of(axis, before, after)
    far = {bits: swapped(side, axis, bits) for bits, side in ((2, side2), (4, side4), (6, side4))}
    mine = stacked(*(own[bits] for bits in (0, *cross)), side1)
    theirs = swapped(mine, axis, 1)
    one = (None,)
    direct = [own[bits] for bits in (0, *cross)] + [before, after] + [far[bits] for bits in cross]
    direct = [(block, one) for block in direct]
    swaps = [(theirs, tuple(range(WIN // 2 + 1)))]
    late = [(swapped(far[bits], axis, 1), one) for bits in cross]
    total = block_sum(0, inter, factors, [total], direct)
    total = block_sum(len(direct), inter, factors, [total], swaps)
    late_first = len(direct) + WIN // 2 + 1
    if aux_count == 1:
        residual, updated = block_sum(late_first, inter, factors, [total], late, (scale, masked))
        return residual[None], updated[None]

    partial_sum = block_sum(late_first, inter, factors, [total], late)[None]
    pno_width = amplitudes.shape[1]
    row_span = pno_width // aux_count
    first_row = lax.axis_index("aux") * row_span
    live_rows = jnp.arange(pno_width)[None, :] < ranks[:, None]
    square_mask = live_rows[:, :, None] & live_rows[:, None, :]
    summed = lax.psum_scatter(partial_sum, "aux", scatter_dimension=1, tiled=True)
    row_energy = lax.dynamic_slice_in_dim(energies, first_row, row_span, 1)
    denominator = row_energy[:, :, None] + energies[:, None, :]
    row_amp = lax.dynamic_slice_in_dim(masked[None], first_row, row_span, 1).astype(F32)
    row_mask = lax.dynamic_slice_in_dim(square_mask, first_row, row_span, 1)
    residual = jnp.where(row_mask, summed + denominator * row_amp, jnp.zeros((), F32))
    return (residual, row_amp - residual / denominator)


def solution(mesh):
    return jax.shard_map(
        shards,
        mesh=mesh,
        in_specs=(
            P("pair", None, None),
            P("pair"),
            P("pair", "aux"),
            P("pair", "aux", None, None),
            P("pair", "aux"),
            P("pair", None),
            P("pair", None, "aux", None),
        ),
        out_specs=(P("pair", "aux", None), P("pair", "aux", None)),
        check_vma=False,
    )
```

```python
import functools

import jax
import jax.numpy as jnp
from jax import lax
from jax.experimental import pallas as pl
from jax.experimental.pallas import tpu as pltpu
from jax.sharding import PartitionSpec as P

WIN = 8
F32 = jnp.float32
BF16 = jnp.bfloat16
VMEM = pl.BlockSpec(memory_space=pltpu.VMEM)
CHUNKS = 5
STAGE_COST = 8
EXCHANGE_COST = 8
TILE = (8, 128)
SMEM = pl.BlockSpec(memory_space=pltpu.SMEM)
ANY = pl.BlockSpec(memory_space=pl.ANY)
PARAMS = pltpu.CompilerParams(vmem_limit_bytes=4 << 20)


def permuted(value, axis, target):
    count = lax.axis_size(axis)
    return lax.ppermute(value, axis, [(source, target(source)) for source in range(count)])


def swapped(value, axis, bits):
    return permuted(value, axis, lambda source: source ^ bits)


def shifted(value, axis, steps):
    count = lax.axis_size(axis)
    return permuted(value, axis, lambda source: (source + steps) % count)


def top_bit(number):
    return 1 << (number.bit_length() - 1)


def held(*arrays):
    return [pltpu.with_memory_space_constraint(array, pltpu.VMEM) for array in arrays]


def live_square(rank, shape):
    rows = lax.broadcasted_iota(jnp.int32, shape, 0)
    columns = lax.broadcasted_iota(jnp.int32, shape, 1)
    return jnp.maximum(rows, columns) < rank


def cost(count, width):
    return pl.CostEstimate(
        flops=4 * count * width**3, bytes_accessed=4 * count * width**2, transcendentals=0
    )


def mask_kernel(rank, amplitude, masked, tile):
    square = live_square(rank[...], amplitude.shape)
    masked[...] = jnp.where(square, amplitude[...].astype(F32), 0.0).astype(BF16)
    tile[...] = jnp.broadcast_to(rank[...], tile.shape)


def mask(ranks, amplitude):
    return pl.pallas_call(
        mask_kernel,
        out_shape=(pltpu.VMEM(amplitude.shape, BF16), pltpu.VMEM(TILE, jnp.int32)),
        in_specs=[VMEM, VMEM],
        out_specs=(VMEM, VMEM),
    )(ranks[None], amplitude)


def sides_kernel(axis, before, after, *sides):
    me = lax.axis_index(axis)
    for bits, side in zip((1, 2, 4), sides):
        side[...] = jnp.where((me & bits) != 0, before[...], after[...])


def sides_of(axis, before, after):
    return pl.pallas_call(
        functools.partial(sides_kernel, axis),
        out_shape=(pltpu.VMEM(before.shape, BF16),) * 3,
        in_specs=[VMEM] * 2,
        out_specs=(VMEM,) * 3,
        compiler_params=PARAMS,
    )(*held(before, after))


def pass_kernel(block, again):
    again[...] = block[...]


def passed(block, weight):
    return pl.pallas_call(
        pass_kernel,
        out_shape=pltpu.VMEM(block.shape, BF16),
        in_specs=[VMEM],
        out_specs=VMEM,
        compiler_params=PARAMS,
        cost_estimate=cost(weight, block.shape[0]),
    )(*held(block))


def stack_kernel(*refs):
    for position, block in enumerate(refs[:-1]):
        refs[-1][position] = block[...]


def stacked(*blocks):
    return pl.pallas_call(
        stack_kernel,
        out_shape=pltpu.VMEM((len(blocks), *blocks[0].shape), BF16),
        in_specs=[VMEM] * len(blocks),
        out_specs=VMEM,
        compiler_params=PARAMS,
    )(*held(*blocks))


def one_term(inter, block, factor):
    half = jnp.dot(inter, block, preferred_element_type=F32).astype(BF16)
    projected = lax.dot_general(
        half, inter, (((1,), (1,)), ((), ())), preferred_element_type=F32
    )
    return factor * projected


def far_step(me, bits):
    other = me ^ bits
    return jnp.where(other > me, other - me, other - me + 2 * WIN)


def block_steps(me):
    cross = range(2, WIN, 2)
    steps = [(me ^ bits) - me + WIN for bits in (0, *cross)]
    steps += [0, 2 * WIN]
    steps += [far_step(me, bits) for bits in cross]
    steps += [(me ^ bits) - me + WIN for bits in range(1, WIN, 2)]
    return steps + [far_step(me, bits) for bits in range(1, WIN, 2)]


def stage_kernel(
    whole, axis, rank, masked, neighbours, couplings, energies, inter,
    total, scale, staged, factor,
    near, couple, energy, places, factors, used, small_sems, sems,
):
    small_copies = [
        pltpu.make_async_copy(source, target, small_sems.at[k])
        for k, (source, target) in enumerate(
            ((neighbours, near), (couplings, couple), (energies, energy))
        )
    ]
    for copy in small_copies:
        copy.start()
    count = lax.axis_size(axis)
    me = lax.axis_index(axis)
    slots, blocks = near.shape[1], staged.shape[0]
    for position, step in enumerate(block_steps(me)):
        places[step] = position
        factors[position] = jnp.float32(0)
        used[position] = 0
    for copy in small_copies:
        copy.wait()
    copies = []
    for slot in range(slots):
        step = near[0, slot] - me + WIN
        step = jnp.where(step < 0, step + count, step)
        position = places[jnp.where(step >= count, step - count, step)]
        factors[position] = couple[0, slot]
        used[position] = 1
        copies.append(pltpu.make_async_copy(inter.at[slot], staged.at[position], sems.at[slot]))
        copies[-1].start()
    along = jnp.broadcast_to(energy[...], total.shape)
    denominator = along + along.T
    if whole:
        total[...] = denominator * masked[...].astype(F32)
    else:
        total[...] = jnp.zeros_like(total)
    scale[...] = jnp.where(live_square(rank[0:1, 0:1], total.shape), 1.0 / denominator, 0.0)
    for position in range(blocks):

        @pl.when(used[position] == 0)
        def _():
            staged[position] = jnp.zeros(staged.shape[1:], BF16)

        factor[position] = jnp.full(factor.shape[1:], factors[position], F32)
    for copy in copies:
        copy.wait()


def stage(whole, axis, rank, masked, neighbours, couplings, energies, inter):
    blocks, width = 2 * WIN + 1, masked.shape[0]
    square = pltpu.VMEM((width, width), F32)
    arrays = [
        pltpu.with_memory_space_constraint(array, pltpu.HBM)
        for array in (neighbours, couplings, energies, inter)
    ]
    return pl.pallas_call(
        functools.partial(stage_kernel, whole, axis),
        out_shape=(
            square,
            square,
            pltpu.VMEM((blocks, width, width), BF16),
            pltpu.VMEM((blocks, 1, width), F32),
        ),
        in_specs=[VMEM] * 2 + [ANY] * len(arrays),
        out_specs=(VMEM,) * 4,
        scratch_shapes=[
            pltpu.SMEM(neighbours.shape, jnp.int32),
            pltpu.SMEM(couplings.shape, F32),
            pltpu.VMEM(energies.shape, F32),
            pltpu.SMEM((blocks,), jnp.int32),
            pltpu.SMEM((blocks,), F32),
            pltpu.SMEM((blocks,), jnp.int32),
            pltpu.SemaphoreType.DMA((3,)),
            pltpu.SemaphoreType.DMA((neighbours.shape[1],)),
        ],
        compiler_params=PARAMS,
        cost_estimate=cost(STAGE_COST, width),
    )(*held(rank, masked), *arrays)


def exchange_kernel(integrals, total, held_integrals, sems):
    chunks, span = held_integrals.shape[1:3]
    copies = [
        [
            pltpu.make_async_copy(
                integrals.at[side, pl.ds(chunk * span, span)],
                held_integrals.at[side, chunk],
                sems.at[side, chunk],
            )
            for side in range(2)
        ]
        for chunk in range(chunks)
    ]
    for pair in copies:
        for copy in pair:
            copy.start()
    sum_now = jnp.zeros(total.shape, F32)
    for chunk, pair in enumerate(copies):
        for copy in pair:
            copy.wait()
        sum_now = sum_now + lax.dot_general(
            held_integrals[0, chunk], held_integrals[1, chunk], (((0,), (0,)), ((), ())),
            preferred_element_type=F32,
        )
    total[...] = sum_now


def exchange_of(integrals):
    rows, width = integrals.shape[1:]
    integrals = pltpu.with_memory_space_constraint(integrals, pltpu.HBM)
    return pl.pallas_call(
        exchange_kernel,
        out_shape=pltpu.VMEM((width, width), F32),
        in_specs=[ANY],
        out_specs=VMEM,
        scratch_shapes=[
            pltpu.VMEM((2, CHUNKS, rows // CHUNKS, width), BF16),
            pltpu.SemaphoreType.DMA((2, CHUNKS)),
        ],
        compiler_params=pltpu.CompilerParams(vmem_limit_bytes=8 << 20),
        cost_estimate=cost(EXCHANGE_COST, width),
    )(integrals)


def sum_kernel(first, picks, starts, inter, factors, *refs):
    sum_now = refs[0][...]
    for ref in refs[1:starts]:
        sum_now = sum_now + ref[...]
    refs = refs[starts:]
    position = first
    for ref, pick in zip(refs, picks):
        for index in pick:
            block = ref[...] if index is None else ref[index]
            sum_now = sum_now + one_term(inter[position], block, factors[position])
            position += 1
    refs = refs[len(picks) :]
    if len(refs) == 1:
        refs[0][...] = sum_now
    else:
        scale, masked, residual, updated = refs
        residual[...] = jnp.where(scale[...] > 0, sum_now, 0.0)
        updated[...] = masked[...].astype(F32) - sum_now * scale[...]


def block_sum(first, inter, factors, starts, blocks, ending=()):
    shape = starts[0].shape
    out_shape = pltpu.VMEM(shape, F32)
    if ending:
        out_shape = (jax.ShapeDtypeStruct(shape, F32),) * 2
    picks = [pick for _, pick in blocks]
    arrays = held(inter, factors, *starts, *(block for block, _ in blocks), *ending)
    return pl.pallas_call(
        functools.partial(sum_kernel, first, picks, len(starts)),
        out_shape=out_shape,
        in_specs=[VMEM] * len(arrays),
        out_specs=(VMEM, VMEM) if ending else VMEM,
        compiler_params=PARAMS,
        cost_estimate=cost(sum(map(len, picks)) * (1 if ending or first else 32), shape[0]),
    )(*arrays)


def shards(amplitudes, ranks, neighbours, intersections, couplings, energies, pair_factors):
    aux_count = lax.axis_size("aux")
    axis = "pair"
    count = lax.axis_size(axis)
    masked, rank = mask(ranks, amplitudes[0])
    cross = range(2, WIN, 2)

    own = {0: masked}
    for bits in reversed(cross):
        own[bits] = swapped(masked, axis, bits)
    own[6] = passed(own[6], 4)
    after = shifted(masked, axis, -WIN)
    before = shifted(masked, axis, WIN)
    staged = stage(
        aux_count == 1, axis, rank, masked, neighbours, couplings, energies, intersections[0]
    )
    exchange = exchange_of(pair_factors[0])
    before, after, staged = lax.optimization_barrier((before, after, staged))
    total, scale, inter, factors = staged
    side1, side2, side4 = sides_of(axis, before, after)
    far = {bits: swapped(side, axis, bits) for bits, side in ((2, side2), (4, side4), (6, side4))}
    far[6] = passed(far[6], 4)
    mine = stacked(*(own[bits] for bits in (0, *cross)), side1)
    theirs = swapped(mine, axis, 1)
    one = (None,)
    direct = [own[bits] for bits in (0, *cross)] + [before, after] + [far[bits] for bits in cross]
    direct = [(block, one) for block in direct]
    swaps = [(theirs, tuple(range(WIN // 2 + 1)))]
    late = [(swapped(far[bits], axis, 1), one) for bits in cross]
    total = block_sum(0, inter, factors, [exchange, total], direct)
    total = block_sum(len(direct), inter, factors, [total], swaps)
    late_first = len(direct) + WIN // 2 + 1
    if aux_count == 1:
        residual, updated = block_sum(late_first, inter, factors, [total], late, (scale, masked))
        return residual[None], updated[None]

    partial_sum = block_sum(late_first, inter, factors, [total], late)[None]
    pno_width = amplitudes.shape[1]
    row_span = pno_width // aux_count
    first_row = lax.axis_index("aux") * row_span
    live_rows = jnp.arange(pno_width)[None, :] < ranks[:, None]
    square_mask = live_rows[:, :, None] & live_rows[:, None, :]
    summed = lax.psum_scatter(partial_sum, "aux", scatter_dimension=1, tiled=True)
    row_energy = lax.dynamic_slice_in_dim(energies, first_row, row_span, 1)
    denominator = row_energy[:, :, None] + energies[:, None, :]
    row_amp = lax.dynamic_slice_in_dim(masked[None], first_row, row_span, 1).astype(F32)
    row_mask = lax.dynamic_slice_in_dim(square_mask, first_row, row_span, 1)
    residual = jnp.where(row_mask, summed + denominator * row_amp, jnp.zeros((), F32))
    return (residual, row_amp - residual / denominator)


def solution(mesh):
    return jax.shard_map(
        shards,
        mesh=mesh,
        in_specs=(
            P("pair", None, None),
            P("pair"),
            P("pair", "aux"),
            P("pair", "aux", None, None),
            P("pair", "aux"),
            P("pair", None),
            P("pair", None, "aux", None),
        ),
        out_specs=(P("pair", "aux", None), P("pair", "aux", None)),
        check_vma=False,
    )
```

```python
import functools

import jax
import jax.numpy as jnp
from jax import lax
from jax.experimental import pallas as pl
from jax.experimental.pallas import tpu as pltpu
from jax.sharding import PartitionSpec as P

WIN = 8
F32 = jnp.float32
BF16 = jnp.bfloat16
VMEM = pl.BlockSpec(memory_space=pltpu.VMEM)
CHUNKS = 5
STAGE_COST = 8
EXCHANGE_COST = 8
TILE = (8, 128)
SMEM = pl.BlockSpec(memory_space=pltpu.SMEM)
ANY = pl.BlockSpec(memory_space=pl.ANY)
PARAMS = pltpu.CompilerParams(vmem_limit_bytes=4 << 20)


def permuted(value, axis, target):
    count = lax.axis_size(axis)
    return lax.ppermute(value, axis, [(source, target(source)) for source in range(count)])


def swapped(value, axis, bits):
    return permuted(value, axis, lambda source: source ^ bits)


def shifted(value, axis, steps):
    count = lax.axis_size(axis)
    return permuted(value, axis, lambda source: (source + steps) % count)


def top_bit(number):
    return 1 << (number.bit_length() - 1)


def held(*arrays):
    return [pltpu.with_memory_space_constraint(array, pltpu.VMEM) for array in arrays]


def live_square(rank, shape):
    rows = lax.broadcasted_iota(jnp.int32, shape, 0)
    columns = lax.broadcasted_iota(jnp.int32, shape, 1)
    return jnp.maximum(rows, columns) < rank


def cost(count, width):
    return pl.CostEstimate(
        flops=4 * count * width**3, bytes_accessed=4 * count * width**2, transcendentals=0
    )


def mask_kernel(rank, amplitude, masked, tile):
    square = live_square(rank[...], amplitude.shape)
    masked[...] = jnp.where(square, amplitude[...].astype(F32), 0.0).astype(BF16)
    tile[...] = jnp.broadcast_to(rank[...], tile.shape)


def mask(ranks, amplitude):
    return pl.pallas_call(
        mask_kernel,
        out_shape=(pltpu.VMEM(amplitude.shape, BF16), pltpu.VMEM(TILE, jnp.int32)),
        in_specs=[VMEM, VMEM],
        out_specs=(VMEM, VMEM),
    )(ranks[None], amplitude)


def sides_kernel(axis, before, after, *sides):
    me = lax.axis_index(axis)
    for bits, side in zip((1, 2, 4), sides):
        side[...] = jnp.where((me & bits) != 0, before[...], after[...])


def sides_of(axis, before, after):
    return pl.pallas_call(
        functools.partial(sides_kernel, axis),
        out_shape=(pltpu.VMEM(before.shape, BF16),) * 3,
        in_specs=[VMEM] * 2,
        out_specs=(VMEM,) * 3,
        compiler_params=PARAMS,
    )(*held(before, after))


def pass_kernel(block, again):
    again[...] = block[...]


def passed(block, weight):
    return pl.pallas_call(
        pass_kernel,
        out_shape=pltpu.VMEM(block.shape, BF16),
        in_specs=[VMEM],
        out_specs=VMEM,
        compiler_params=PARAMS,
        cost_estimate=cost(weight, block.shape[0]),
    )(*held(block))


def stack_kernel(*refs):
    for position, block in enumerate(refs[:-1]):
        refs[-1][position] = block[...]


def stacked(*blocks):
    return pl.pallas_call(
        stack_kernel,
        out_shape=pltpu.VMEM((len(blocks), *blocks[0].shape), BF16),
        in_specs=[VMEM] * len(blocks),
        out_specs=VMEM,
        compiler_params=PARAMS,
    )(*held(*blocks))


def one_term(inter, block, factor):
    half = jnp.dot(inter, block, preferred_element_type=F32).astype(BF16)
    projected = lax.dot_general(
        half, inter, (((1,), (1,)), ((), ())), preferred_element_type=F32
    )
    return factor * projected


def far_step(me, bits):
    other = me ^ bits
    return jnp.where(other > me, other - me, other - me + 2 * WIN)


def block_steps(me):
    cross = range(2, WIN, 2)
    steps = [(me ^ bits) - me + WIN for bits in (0, *cross)]
    steps += [0, 2 * WIN]
    steps += [far_step(me, bits) for bits in (6, 2, 4)]
    steps += [(me ^ bits) - me + WIN for bits in range(1, WIN, 2)]
    return steps + [far_step(me, bits) for bits in range(1, WIN, 2)]


def stage_kernel(
    whole, axis, rank, masked, neighbours, couplings, energies, inter,
    total, scale, staged, factor,
    near, couple, energy, places, factors, used, small_sems, sems,
):
    small_copies = [
        pltpu.make_async_copy(source, target, small_sems.at[k])
        for k, (source, target) in enumerate(
            ((neighbours, near), (couplings, couple), (energies, energy))
        )
    ]
    for copy in small_copies:
        copy.start()
    count = lax.axis_size(axis)
    me = lax.axis_index(axis)
    slots, blocks = near.shape[1], staged.shape[0]
    for position, step in enumerate(block_steps(me)):
        places[step] = position
        factors[position] = jnp.float32(0)
        used[position] = 0
    for copy in small_copies:
        copy.wait()
    copies = []
    for slot in range(slots):
        step = near[0, slot] - me + WIN
        step = jnp.where(step < 0, step + count, step)
        position = places[jnp.where(step >= count, step - count, step)]
        factors[position] = couple[0, slot]
        used[position] = 1
        copies.append(pltpu.make_async_copy(inter.at[slot], staged.at[position], sems.at[slot]))
        copies[-1].start()
    along = jnp.broadcast_to(energy[...], total.shape)
    denominator = along + along.T
    if whole:
        total[...] = denominator * masked[...].astype(F32)
    else:
        total[...] = jnp.zeros_like(total)
    scale[...] = jnp.where(live_square(rank[0:1, 0:1], total.shape), 1.0 / denominator, 0.0)
    for position in range(blocks):

        @pl.when(used[position] == 0)
        def _():
            staged[position] = jnp.zeros(staged.shape[1:], BF16)

        factor[position] = jnp.full(factor.shape[1:], factors[position], F32)
    for copy in copies:
        copy.wait()


def stage(whole, axis, rank, masked, neighbours, couplings, energies, inter):
    blocks, width = 2 * WIN + 1, masked.shape[0]
    square = pltpu.VMEM((width, width), F32)
    arrays = [
        pltpu.with_memory_space_constraint(array, pltpu.HBM)
        for array in (neighbours, couplings, energies, inter)
    ]
    return pl.pallas_call(
        functools.partial(stage_kernel, whole, axis),
        out_shape=(
            square,
            square,
            pltpu.VMEM((blocks, width, width), BF16),
            pltpu.VMEM((blocks, 1, width), F32),
        ),
        in_specs=[VMEM] * 2 + [ANY] * len(arrays),
        out_specs=(VMEM,) * 4,
        scratch_shapes=[
            pltpu.SMEM(neighbours.shape, jnp.int32),
            pltpu.SMEM(couplings.shape, F32),
            pltpu.VMEM(energies.shape, F32),
            pltpu.SMEM((blocks,), jnp.int32),
            pltpu.SMEM((blocks,), F32),
            pltpu.SMEM((blocks,), jnp.int32),
            pltpu.SemaphoreType.DMA((3,)),
            pltpu.SemaphoreType.DMA((neighbours.shape[1],)),
        ],
        compiler_params=PARAMS,
        cost_estimate=cost(STAGE_COST, width),
    )(*held(rank, masked), *arrays)


def exchange_kernel(integrals, total, held_integrals, sems):
    chunks, span = held_integrals.shape[1:3]
    copies = [
        [
            pltpu.make_async_copy(
                integrals.at[side, pl.ds(chunk * span, span)],
                held_integrals.at[side, chunk],
                sems.at[side, chunk],
            )
            for side in range(2)
        ]
        for chunk in range(chunks)
    ]
    for pair in copies:
        for copy in pair:
            copy.start()
    sum_now = jnp.zeros(total.shape, F32)
    for chunk, pair in enumerate(copies):
        for copy in pair:
            copy.wait()
        sum_now = sum_now + lax.dot_general(
            held_integrals[0, chunk], held_integrals[1, chunk], (((0,), (0,)), ((), ())),
            preferred_element_type=F32,
        )
    total[...] = sum_now


def exchange_of(integrals):
    rows, width = integrals.shape[1:]
    integrals = pltpu.with_memory_space_constraint(integrals, pltpu.HBM)
    return pl.pallas_call(
        exchange_kernel,
        out_shape=pltpu.VMEM((width, width), F32),
        in_specs=[ANY],
        out_specs=VMEM,
        scratch_shapes=[
            pltpu.VMEM((2, CHUNKS, rows // CHUNKS, width), BF16),
            pltpu.SemaphoreType.DMA((2, CHUNKS)),
        ],
        compiler_params=pltpu.CompilerParams(vmem_limit_bytes=8 << 20),
        cost_estimate=cost(EXCHANGE_COST, width),
    )(integrals)


def sum_kernel(first, picks, starts, inter, factors, *refs):
    sum_now = refs[0][...]
    for ref in refs[1:starts]:
        sum_now = sum_now + ref[...]
    refs = refs[starts:]
    position = first
    for ref, pick in zip(refs, picks):
        for index in pick:
            block = ref[...] if index is None else ref[index]
            sum_now = sum_now + one_term(inter[position], block, factors[position])
            position += 1
    refs = refs[len(picks) :]
    if len(refs) == 1:
        refs[0][...] = sum_now
    else:
        scale, masked, residual, updated = refs
        residual[...] = jnp.where(scale[...] > 0, sum_now, 0.0)
        updated[...] = masked[...].astype(F32) - sum_now * scale[...]


def block_sum(first, inter, factors, starts, blocks, weight=1, ending=()):
    shape = starts[0].shape
    out_shape = pltpu.VMEM(shape, F32)
    if ending:
        out_shape = (jax.ShapeDtypeStruct(shape, F32),) * 2
    picks = [pick for _, pick in blocks]
    arrays = held(inter, factors, *starts, *(block for block, _ in blocks), *ending)
    return pl.pallas_call(
        functools.partial(sum_kernel, first, picks, len(starts)),
        out_shape=out_shape,
        in_specs=[VMEM] * len(arrays),
        out_specs=(VMEM, VMEM) if ending else VMEM,
        compiler_params=PARAMS,
        cost_estimate=cost(sum(map(len, picks)) * weight, shape[0]),
    )(*arrays)


def shards(amplitudes, ranks, neighbours, intersections, couplings, energies, pair_factors):
    aux_count = lax.axis_size("aux")
    axis = "pair"
    count = lax.axis_size(axis)
    masked, rank = mask(ranks, amplitudes[0])
    cross = range(2, WIN, 2)

    own = {0: masked}
    for bits in reversed(cross):
        own[bits] = swapped(masked, axis, bits)
    own[6] = passed(own[6], 4)
    after = shifted(masked, axis, -WIN)
    before = shifted(masked, axis, WIN)
    staged = stage(
        aux_count == 1, axis, rank, masked, neighbours, couplings, energies, intersections[0]
    )
    exchange = exchange_of(pair_factors[0])
    after, before, staged = lax.optimization_barrier((after, before, staged))
    total, scale, inter, factors = staged
    side1, side2, side4 = sides_of(axis, before, after)
    far = {bits: swapped(side, axis, bits) for bits, side in ((2, side2), (4, side4), (6, side4))}
    far[6] = passed(far[6], 4)
    mine = stacked(*(own[bits] for bits in (0, *cross)), side1)
    theirs = swapped(mine, axis, 1)
    one = (None,)
    near = [own[bits] for bits in (0, *cross)] + [before, after, far[6]]
    near = [(block, one) for block in near]
    total = block_sum(0, inter, factors, [exchange, total], near, 1)
    far[2], far[4], total = lax.optimization_barrier((far[2], far[4], total))
    late = [(swapped(far[bits], axis, 1), one) for bits in cross]
    total = block_sum(len(near), inter, factors, [total], [(far[2], one), (far[4], one)], 64)
    total = block_sum(len(near) + 2, inter, factors, [total], [(theirs, tuple(range(WIN // 2 + 1)))], 32)
    late_first = len(near) + 2 + WIN // 2 + 1
    if aux_count == 1:
        residual, updated = block_sum(late_first, inter, factors, [total], late, ending=(scale, masked))
        return residual[None], updated[None]

    partial_sum = block_sum(late_first, inter, factors, [total], late)[None]
    pno_width = amplitudes.shape[1]
    row_span = pno_width // aux_count
    first_row = lax.axis_index("aux") * row_span
    live_rows = jnp.arange(pno_width)[None, :] < ranks[:, None]
    square_mask = live_rows[:, :, None] & live_rows[:, None, :]
    summed = lax.psum_scatter(partial_sum, "aux", scatter_dimension=1, tiled=True)
    row_energy = lax.dynamic_slice_in_dim(energies, first_row, row_span, 1)
    denominator = row_energy[:, :, None] + energies[:, None, :]
    row_amp = lax.dynamic_slice_in_dim(masked[None], first_row, row_span, 1).astype(F32)
    row_mask = lax.dynamic_slice_in_dim(square_mask, first_row, row_span, 1)
    residual = jnp.where(row_mask, summed + denominator * row_amp, jnp.zeros((), F32))
    return (residual, row_amp - residual / denominator)


def solution(mesh):
    return jax.shard_map(
        shards,
        mesh=mesh,
        in_specs=(
            P("pair", None, None),
            P("pair"),
            P("pair", "aux"),
            P("pair", "aux", None, None),
            P("pair", "aux"),
            P("pair", None),
            P("pair", None, "aux", None),
        ),
        out_specs=(P("pair", "aux", None), P("pair", "aux", None)),
        check_vma=False,
    )
```

```python
import functools

import jax
import jax.numpy as jnp
from jax import lax
from jax.experimental import pallas as pl
from jax.experimental.pallas import tpu as pltpu
from jax.sharding import PartitionSpec as P

WIN = 8
F32 = jnp.float32
BF16 = jnp.bfloat16
VMEM = pl.BlockSpec(memory_space=pltpu.VMEM)
CHUNKS = 5
STAGE_COST = 8
EXCHANGE_COST = 8
TILE = (8, 128)
SMEM = pl.BlockSpec(memory_space=pltpu.SMEM)
ANY = pl.BlockSpec(memory_space=pl.ANY)
PARAMS = pltpu.CompilerParams(vmem_limit_bytes=4 << 20)


def permuted(value, axis, target):
    count = lax.axis_size(axis)
    return lax.ppermute(value, axis, [(source, target(source)) for source in range(count)])


def swapped(value, axis, bits):
    return permuted(value, axis, lambda source: source ^ bits)


def shifted(value, axis, steps):
    count = lax.axis_size(axis)
    return permuted(value, axis, lambda source: (source + steps) % count)


def top_bit(number):
    return 1 << (number.bit_length() - 1)


def held(*arrays):
    return [pltpu.with_memory_space_constraint(array, pltpu.VMEM) for array in arrays]


def live_square(rank, shape):
    rows = lax.broadcasted_iota(jnp.int32, shape, 0)
    columns = lax.broadcasted_iota(jnp.int32, shape, 1)
    return jnp.maximum(rows, columns) < rank


def cost(count, width):
    return pl.CostEstimate(
        flops=4 * count * width**3, bytes_accessed=4 * count * width**2, transcendentals=0
    )


def mask_kernel(rank, amplitude, masked, tile):
    square = live_square(rank[...], amplitude.shape)
    masked[...] = jnp.where(square, amplitude[...].astype(F32), 0.0).astype(BF16)
    tile[...] = jnp.broadcast_to(rank[...], tile.shape)


def mask(ranks, amplitude):
    return pl.pallas_call(
        mask_kernel,
        out_shape=(pltpu.VMEM(amplitude.shape, BF16), pltpu.VMEM(TILE, jnp.int32)),
        in_specs=[VMEM, VMEM],
        out_specs=(VMEM, VMEM),
    )(ranks[None], amplitude)


def sides_kernel(axis, before, after, *sides):
    me = lax.axis_index(axis)
    for bits, side in zip((1, 2, 4), sides):
        side[...] = jnp.where((me & bits) != 0, before[...], after[...])


def sides_of(axis, before, after):
    return pl.pallas_call(
        functools.partial(sides_kernel, axis),
        out_shape=(pltpu.VMEM(before.shape, BF16),) * 3,
        in_specs=[VMEM] * 2,
        out_specs=(VMEM,) * 3,
        compiler_params=PARAMS,
    )(*held(before, after))


def pass_kernel(block, again):
    again[...] = block[...]


def passed(block, weight):
    return pl.pallas_call(
        pass_kernel,
        out_shape=pltpu.VMEM(block.shape, BF16),
        in_specs=[VMEM],
        out_specs=VMEM,
        compiler_params=PARAMS,
        cost_estimate=cost(weight, block.shape[0]),
    )(*held(block))


def stack_kernel(*refs):
    for position, block in enumerate(refs[:-1]):
        refs[-1][position] = block[...]


def stacked(*blocks):
    return pl.pallas_call(
        stack_kernel,
        out_shape=pltpu.VMEM((len(blocks), *blocks[0].shape), BF16),
        in_specs=[VMEM] * len(blocks),
        out_specs=VMEM,
        compiler_params=PARAMS,
    )(*held(*blocks))


def one_term(inter, block, factor):
    half = jnp.dot(inter, block, preferred_element_type=F32).astype(BF16)
    projected = lax.dot_general(
        half, inter, (((1,), (1,)), ((), ())), preferred_element_type=F32
    )
    return factor * projected


def far_step(me, bits):
    other = me ^ bits
    return jnp.where(other > me, other - me, other - me + 2 * WIN)


def block_steps(me):
    cross = range(2, WIN, 2)
    steps = [(me ^ bits) - me + WIN for bits in (0, *cross)]
    steps += [0, 2 * WIN]
    steps += [far_step(me, bits) for bits in (6, 2, 4)]
    steps += [(me ^ bits) - me + WIN for bits in range(1, WIN, 2)]
    return steps + [far_step(me, bits) for bits in (1, 7, 3, 5)]


def stage_kernel(
    whole, axis, rank, masked, neighbours, couplings, energies, inter,
    total, scale, staged, factor,
    near, couple, energy, places, factors, used, small_sems, sems,
):
    small_copies = [
        pltpu.make_async_copy(source, target, small_sems.at[k])
        for k, (source, target) in enumerate(
            ((neighbours, near), (couplings, couple), (energies, energy))
        )
    ]
    for copy in small_copies:
        copy.start()
    count = lax.axis_size(axis)
    me = lax.axis_index(axis)
    slots, blocks = near.shape[1], staged.shape[0]
    for position, step in enumerate(block_steps(me)):
        places[step] = position
        factors[position] = jnp.float32(0)
        used[position] = 0
    for copy in small_copies:
        copy.wait()
    copies = []
    for slot in range(slots):
        step = near[0, slot] - me + WIN
        step = jnp.where(step < 0, step + count, step)
        position = places[jnp.where(step >= count, step - count, step)]
        factors[position] = couple[0, slot]
        used[position] = 1
        copies.append(pltpu.make_async_copy(inter.at[slot], staged.at[position], sems.at[slot]))
        copies[-1].start()
    along = jnp.broadcast_to(energy[...], total.shape)
    denominator = along + along.T
    if whole:
        total[...] = denominator * masked[...].astype(F32)
    else:
        total[...] = jnp.zeros_like(total)
    scale[...] = jnp.where(live_square(rank[0:1, 0:1], total.shape), 1.0 / denominator, 0.0)
    for position in range(blocks):

        @pl.when(used[position] == 0)
        def _():
            staged[position] = jnp.zeros(staged.shape[1:], BF16)

        factor[position] = jnp.full(factor.shape[1:], factors[position], F32)
    for copy in copies:
        copy.wait()


def stage(whole, axis, rank, masked, neighbours, couplings, energies, inter):
    blocks, width = 2 * WIN + 1, masked.shape[0]
    square = pltpu.VMEM((width, width), F32)
    arrays = [
        pltpu.with_memory_space_constraint(array, pltpu.HBM)
        for array in (neighbours, couplings, energies, inter)
    ]
    return pl.pallas_call(
        functools.partial(stage_kernel, whole, axis),
        out_shape=(
            square,
            square,
            pltpu.VMEM((blocks, width, width), BF16),
            pltpu.VMEM((blocks, 1, width), F32),
        ),
        in_specs=[VMEM] * 2 + [ANY] * len(arrays),
        out_specs=(VMEM,) * 4,
        scratch_shapes=[
            pltpu.SMEM(neighbours.shape, jnp.int32),
            pltpu.SMEM(couplings.shape, F32),
            pltpu.VMEM(energies.shape, F32),
            pltpu.SMEM((blocks,), jnp.int32),
            pltpu.SMEM((blocks,), F32),
            pltpu.SMEM((blocks,), jnp.int32),
            pltpu.SemaphoreType.DMA((3,)),
            pltpu.SemaphoreType.DMA((neighbours.shape[1],)),
        ],
        compiler_params=PARAMS,
        cost_estimate=cost(STAGE_COST, width),
    )(*held(rank, masked), *arrays)


def exchange_kernel(integrals, total, held_integrals, sems):
    chunks, span = held_integrals.shape[1:3]
    copies = [
        [
            pltpu.make_async_copy(
                integrals.at[side, pl.ds(chunk * span, span)],
                held_integrals.at[side, chunk],
                sems.at[side, chunk],
            )
            for side in range(2)
        ]
        for chunk in range(chunks)
    ]
    for pair in copies:
        for copy in pair:
            copy.start()
    sum_now = jnp.zeros(total.shape, F32)
    for chunk, pair in enumerate(copies):
        for copy in pair:
            copy.wait()
        sum_now = sum_now + lax.dot_general(
            held_integrals[0, chunk], held_integrals[1, chunk], (((0,), (0,)), ((), ())),
            preferred_element_type=F32,
        )
    total[...] = sum_now


def exchange_of(integrals):
    rows, width = integrals.shape[1:]
    integrals = pltpu.with_memory_space_constraint(integrals, pltpu.HBM)
    return pl.pallas_call(
        exchange_kernel,
        out_shape=pltpu.VMEM((width, width), F32),
        in_specs=[ANY],
        out_specs=VMEM,
        scratch_shapes=[
            pltpu.VMEM((2, CHUNKS, rows // CHUNKS, width), BF16),
            pltpu.SemaphoreType.DMA((2, CHUNKS)),
        ],
        compiler_params=pltpu.CompilerParams(vmem_limit_bytes=8 << 20),
        cost_estimate=cost(EXCHANGE_COST, width),
    )(integrals)


def sum_kernel(first, picks, starts, inter, factors, *refs):
    sum_now = refs[0][...]
    for ref in refs[1:starts]:
        sum_now = sum_now + ref[...]
    refs = refs[starts:]
    position = first
    for ref, pick in zip(refs, picks):
        for index in pick:
            block = ref[...] if index is None else ref[index]
            sum_now = sum_now + one_term(inter[position], block, factors[position])
            position += 1
    refs = refs[len(picks) :]
    if len(refs) == 1:
        refs[0][...] = sum_now
    else:
        scale, masked, residual, updated = refs
        residual[...] = jnp.where(scale[...] > 0, sum_now, 0.0)
        updated[...] = masked[...].astype(F32) - sum_now * scale[...]


def block_sum(first, inter, factors, starts, blocks, weight=1, ending=()):
    shape = starts[0].shape
    out_shape = pltpu.VMEM(shape, F32)
    if ending:
        out_shape = (jax.ShapeDtypeStruct(shape, F32),) * 2
    picks = [pick for _, pick in blocks]
    arrays = held(inter, factors, *starts, *(block for block, _ in blocks), *ending)
    return pl.pallas_call(
        functools.partial(sum_kernel, first, picks, len(starts)),
        out_shape=out_shape,
        in_specs=[VMEM] * len(arrays),
        out_specs=(VMEM, VMEM) if ending else VMEM,
        compiler_params=PARAMS,
        cost_estimate=cost(sum(map(len, picks)) * weight, shape[0]),
    )(*arrays)


def shards(amplitudes, ranks, neighbours, intersections, couplings, energies, pair_factors):
    aux_count = lax.axis_size("aux")
    axis = "pair"
    count = lax.axis_size(axis)
    masked, rank = mask(ranks, amplitudes[0])
    cross = range(2, WIN, 2)

    own = {0: masked}
    for bits in reversed(cross):
        own[bits] = swapped(masked, axis, bits)
    own[6] = passed(own[6], 4)
    after = shifted(masked, axis, -WIN)
    before = shifted(masked, axis, WIN)
    staged = stage(
        aux_count == 1, axis, rank, masked, neighbours, couplings, energies, intersections[0]
    )
    exchange = exchange_of(pair_factors[0])
    after, before, staged = lax.optimization_barrier((after, before, staged))
    total, scale, inter, factors = staged
    side1, side2, side4 = sides_of(axis, before, after)
    far = {bits: swapped(side, axis, bits) for bits, side in ((2, side2), (4, side4), (6, side4))}
    far[6] = passed(far[6], 4)
    mine = stacked(*(own[bits] for bits in (0, *cross)), side1)
    theirs = swapped(mine, axis, 1)
    one = (None,)
    near = [own[bits] for bits in (0, *cross)] + [before, after, far[6]]
    near = [(block, one) for block in near]
    total = block_sum(0, inter, factors, [exchange, total], near, 1)
    far[2], far[4], total = lax.optimization_barrier((far[2], far[4], total))
    pair_now = swapped(stacked(far[2], far[4]), axis, 1)
    late = [(pair_now, (0, 1))]
    diagonal = swapped(far[6], axis, 1)
    total = block_sum(len(near), inter, factors, [total], [(far[2], one), (far[4], one)], 64)
    total = block_sum(len(near) + 2, inter, factors, [total], [(theirs, tuple(range(WIN // 2 + 1))), (diagonal, one)], 1)
    late_first = len(near) + 2 + WIN // 2 + 2
    if aux_count == 1:
        residual, updated = block_sum(late_first, inter, factors, [total], late, ending=(scale, masked))
        return residual[None], updated[None]

    partial_sum = block_sum(late_first, inter, factors, [total], late)[None]
    pno_width = amplitudes.shape[1]
    row_span = pno_width // aux_count
    first_row = lax.axis_index("aux") * row_span
    live_rows = jnp.arange(pno_width)[None, :] < ranks[:, None]
    square_mask = live_rows[:, :, None] & live_rows[:, None, :]
    summed = lax.psum_scatter(partial_sum, "aux", scatter_dimension=1, tiled=True)
    row_energy = lax.dynamic_slice_in_dim(energies, first_row, row_span, 1)
    denominator = row_energy[:, :, None] + energies[:, None, :]
    row_amp = lax.dynamic_slice_in_dim(masked[None], first_row, row_span, 1).astype(F32)
    row_mask = lax.dynamic_slice_in_dim(square_mask, first_row, row_span, 1)
    residual = jnp.where(row_mask, summed + denominator * row_amp, jnp.zeros((), F32))
    return (residual, row_amp - residual / denominator)


def solution(mesh):
    return jax.shard_map(
        shards,
        mesh=mesh,
        in_specs=(
            P("pair", None, None),
            P("pair"),
            P("pair", "aux"),
            P("pair", "aux", None, None),
            P("pair", "aux"),
            P("pair", None),
            P("pair", None, "aux", None),
        ),
        out_specs=(P("pair", "aux", None), P("pair", "aux", None)),
        check_vma=False,
    )
```

```python
import functools

import jax
import jax.numpy as jnp
from jax import lax
from jax.experimental import pallas as pl
from jax.experimental.pallas import tpu as pltpu
from jax.sharding import PartitionSpec as P

WIN = 8
F32 = jnp.float32
BF16 = jnp.bfloat16
VMEM = pl.BlockSpec(memory_space=pltpu.VMEM)
CHUNKS = 5
STAGE_COST = 8
EXCHANGE_COST = 8
TILE = (8, 128)
SMEM = pl.BlockSpec(memory_space=pltpu.SMEM)
ANY = pl.BlockSpec(memory_space=pl.ANY)
PARAMS = pltpu.CompilerParams(vmem_limit_bytes=4 << 20)


def permuted(value, axis, target):
    count = lax.axis_size(axis)
    return lax.ppermute(value, axis, [(source, target(source)) for source in range(count)])


def swapped(value, axis, bits):
    return permuted(value, axis, lambda source: source ^ bits)


def shifted(value, axis, steps):
    count = lax.axis_size(axis)
    return permuted(value, axis, lambda source: (source + steps) % count)


def top_bit(number):
    return 1 << (number.bit_length() - 1)


def held(*arrays):
    return [pltpu.with_memory_space_constraint(array, pltpu.VMEM) for array in arrays]


def live_square(rank, shape):
    rows = lax.broadcasted_iota(jnp.int32, shape, 0)
    columns = lax.broadcasted_iota(jnp.int32, shape, 1)
    return jnp.maximum(rows, columns) < rank


def cost(count, width):
    return pl.CostEstimate(
        flops=4 * count * width**3, bytes_accessed=4 * count * width**2, transcendentals=0
    )


def mask_kernel(rank, amplitude, masked, tile):
    square = live_square(rank[...], amplitude.shape)
    masked[...] = jnp.where(square, amplitude[...].astype(F32), 0.0).astype(BF16)
    tile[...] = jnp.broadcast_to(rank[...], tile.shape)


def mask(ranks, amplitude):
    return pl.pallas_call(
        mask_kernel,
        out_shape=(pltpu.VMEM(amplitude.shape, BF16), pltpu.VMEM(TILE, jnp.int32)),
        in_specs=[VMEM, VMEM],
        out_specs=(VMEM, VMEM),
    )(ranks[None], amplitude)


def sides_kernel(axis, before, after, *sides):
    me = lax.axis_index(axis)
    for bits, side in zip((1, 2, 4), sides):
        side[...] = jnp.where((me & bits) != 0, before[...], after[...])


def sides_of(axis, before, after):
    return pl.pallas_call(
        functools.partial(sides_kernel, axis),
        out_shape=(pltpu.VMEM(before.shape, BF16),) * 3,
        in_specs=[VMEM] * 2,
        out_specs=(VMEM,) * 3,
        compiler_params=PARAMS,
    )(*held(before, after))


def pass_kernel(block, again):
    again[...] = block[...]


def passed(block, weight):
    return pl.pallas_call(
        pass_kernel,
        out_shape=pltpu.VMEM(block.shape, BF16),
        in_specs=[VMEM],
        out_specs=VMEM,
        compiler_params=PARAMS,
        cost_estimate=cost(weight, block.shape[0]),
    )(*held(block))


def stack_kernel(*refs):
    for position, block in enumerate(refs[:-1]):
        refs[-1][position] = block[...]


def stacked(*blocks):
    return pl.pallas_call(
        stack_kernel,
        out_shape=pltpu.VMEM((len(blocks), *blocks[0].shape), BF16),
        in_specs=[VMEM] * len(blocks),
        out_specs=VMEM,
        compiler_params=PARAMS,
    )(*held(*blocks))


def one_term(inter, block, factor):
    half = jnp.dot(inter, block, preferred_element_type=F32).astype(BF16)
    projected = lax.dot_general(
        half, inter, (((1,), (1,)), ((), ())), preferred_element_type=F32
    )
    return factor * projected


def far_step(me, bits):
    other = me ^ bits
    return jnp.where(other > me, other - me, other - me + 2 * WIN)


def block_steps(me):
    cross = range(2, WIN, 2)
    steps = [(me ^ bits) - me + WIN for bits in (0, *cross)]
    steps += [0, 2 * WIN]
    steps += [far_step(me, bits) for bits in (6, 2, 4)]
    steps += [(me ^ bits) - me + WIN for bits in range(1, WIN, 2)]
    return steps + [far_step(me, bits) for bits in (1, 7, 3, 5)]


def stage_kernel(
    whole, axis, rank, masked, neighbours, couplings, energies, inter,
    total, scale, staged, factor,
    near, couple, energy, places, factors, used, small_sems, sems,
):
    small_copies = [
        pltpu.make_async_copy(source, target, small_sems.at[k])
        for k, (source, target) in enumerate(
            ((neighbours, near), (couplings, couple), (energies, energy))
        )
    ]
    for copy in small_copies:
        copy.start()
    count = lax.axis_size(axis)
    me = lax.axis_index(axis)
    slots, blocks = near.shape[1], staged.shape[0]
    for position, step in enumerate(block_steps(me)):
        places[step] = position
        factors[position] = jnp.float32(0)
        used[position] = 0
    for copy in small_copies:
        copy.wait()
    copies = []
    for slot in range(slots):
        step = near[0, slot] - me + WIN
        step = jnp.where(step < 0, step + count, step)
        position = places[jnp.where(step >= count, step - count, step)]
        factors[position] = couple[0, slot]
        used[position] = 1
        copies.append(pltpu.make_async_copy(inter.at[slot], staged.at[position], sems.at[slot]))
        copies[-1].start()
    along = jnp.broadcast_to(energy[...], total.shape)
    denominator = along + along.T
    if whole:
        total[...] = denominator * masked[...].astype(F32)
    else:
        total[...] = jnp.zeros_like(total)
    scale[...] = jnp.where(live_square(rank[0:1, 0:1], total.shape), 1.0 / denominator, 0.0)
    for position in range(blocks):

        @pl.when(used[position] == 0)
        def _():
            staged[position] = jnp.zeros(staged.shape[1:], BF16)

        factor[position] = jnp.full(factor.shape[1:], factors[position], F32)
    for copy in copies:
        copy.wait()


def stage(whole, axis, rank, masked, neighbours, couplings, energies, inter):
    blocks, width = 2 * WIN + 1, masked.shape[0]
    square = pltpu.VMEM((width, width), F32)
    arrays = [
        pltpu.with_memory_space_constraint(array, pltpu.HBM)
        for array in (neighbours, couplings, energies, inter)
    ]
    return pl.pallas_call(
        functools.partial(stage_kernel, whole, axis),
        out_shape=(
            square,
            square,
            pltpu.VMEM((blocks, width, width), BF16),
            pltpu.VMEM((blocks, 1, width), F32),
        ),
        in_specs=[VMEM] * 2 + [ANY] * len(arrays),
        out_specs=(VMEM,) * 4,
        scratch_shapes=[
            pltpu.SMEM(neighbours.shape, jnp.int32),
            pltpu.SMEM(couplings.shape, F32),
            pltpu.VMEM(energies.shape, F32),
            pltpu.SMEM((blocks,), jnp.int32),
            pltpu.SMEM((blocks,), F32),
            pltpu.SMEM((blocks,), jnp.int32),
            pltpu.SemaphoreType.DMA((3,)),
            pltpu.SemaphoreType.DMA((neighbours.shape[1],)),
        ],
        compiler_params=PARAMS,
        cost_estimate=cost(STAGE_COST, width),
    )(*held(rank, masked), *arrays)


def exchange_kernel(integrals, total, held_integrals, sems):
    chunks, span = held_integrals.shape[1:3]
    copies = [
        [
            pltpu.make_async_copy(
                integrals.at[side, pl.ds(chunk * span, span)],
                held_integrals.at[side, chunk],
                sems.at[side, chunk],
            )
            for side in range(2)
        ]
        for chunk in range(chunks)
    ]
    for pair in copies:
        for copy in pair:
            copy.start()
    sum_now = jnp.zeros(total.shape, F32)
    for chunk, pair in enumerate(copies):
        for copy in pair:
            copy.wait()
        sum_now = sum_now + lax.dot_general(
            held_integrals[0, chunk], held_integrals[1, chunk], (((0,), (0,)), ((), ())),
            preferred_element_type=F32,
        )
    total[...] = sum_now


def exchange_of(integrals):
    rows, width = integrals.shape[1:]
    integrals = pltpu.with_memory_space_constraint(integrals, pltpu.HBM)
    return pl.pallas_call(
        exchange_kernel,
        out_shape=pltpu.VMEM((width, width), F32),
        in_specs=[ANY],
        out_specs=VMEM,
        scratch_shapes=[
            pltpu.VMEM((2, CHUNKS, rows // CHUNKS, width), BF16),
            pltpu.SemaphoreType.DMA((2, CHUNKS)),
        ],
        compiler_params=pltpu.CompilerParams(vmem_limit_bytes=8 << 20),
        cost_estimate=cost(EXCHANGE_COST, width),
    )(integrals)


def sum_kernel(first, picks, starts, inter, factors, *refs):
    sum_now = refs[0][...]
    for ref in refs[1:starts]:
        sum_now = sum_now + ref[...]
    refs = refs[starts:]
    position = first
    for ref, pick in zip(refs, picks):
        for index in pick:
            block = ref[...] if index is None else ref[index]
            sum_now = sum_now + one_term(inter[position], block, factors[position])
            position += 1
    refs = refs[len(picks) :]
    if len(refs) == 1:
        refs[0][...] = sum_now
    else:
        scale, masked, residual, updated = refs
        residual[...] = jnp.where(scale[...] > 0, sum_now, 0.0)
        updated[...] = masked[...].astype(F32) - sum_now * scale[...]


def block_sum(first, inter, factors, starts, blocks, weight=1, ending=()):
    shape = starts[0].shape
    out_shape = pltpu.VMEM(shape, F32)
    if ending:
        out_shape = (jax.ShapeDtypeStruct(shape, F32),) * 2
    picks = [pick for _, pick in blocks]
    arrays = held(inter, factors, *starts, *(block for block, _ in blocks), *ending)
    return pl.pallas_call(
        functools.partial(sum_kernel, first, picks, len(starts)),
        out_shape=out_shape,
        in_specs=[VMEM] * len(arrays),
        out_specs=(VMEM, VMEM) if ending else VMEM,
        compiler_params=PARAMS,
        cost_estimate=cost(sum(map(len, picks)) * weight, shape[0]),
    )(*arrays)


def shards(amplitudes, ranks, neighbours, intersections, couplings, energies, pair_factors):
    aux_count = lax.axis_size("aux")
    axis = "pair"
    count = lax.axis_size(axis)
    masked, rank = mask(ranks, amplitudes[0])
    cross = range(2, WIN, 2)

    own = {0: masked}
    for bits in reversed(cross):
        own[bits] = swapped(masked, axis, bits)
    own[6] = passed(own[6], 4)
    after = shifted(masked, axis, -WIN)
    before = shifted(masked, axis, WIN)
    staged = stage(
        aux_count == 1, axis, rank, masked, neighbours, couplings, energies, intersections[0]
    )
    before, after, staged = lax.optimization_barrier((before, after, staged))
    total, scale, inter, factors = staged
    side1, side2, side4 = sides_of(axis, before, after)
    far = {bits: swapped(side, axis, bits) for bits, side in ((2, side2), (4, side4), (6, side4))}
    far[6] = passed(far[6], 4)
    mine = stacked(*(own[bits] for bits in (0, *cross)), side1)
    mine, pair_factors = lax.optimization_barrier((mine, pair_factors))
    theirs = swapped(mine, axis, 1)
    exchange = exchange_of(pair_factors[0])
    one = (None,)
    near = [own[bits] for bits in (0, *cross)] + [before, after, far[6]]
    near = [(block, one) for block in near]
    total = block_sum(0, inter, factors, [exchange, total], near, 1)
    far[2], far[4], total = lax.optimization_barrier((far[2], far[4], total))
    pair_now = swapped(stacked(far[2], far[4]), axis, 1)
    late = [(pair_now, (0, 1))]
    diagonal = swapped(far[6], axis, 1)
    total = block_sum(len(near), inter, factors, [total], [(far[2], one), (far[4], one)], 64)
    total = block_sum(len(near) + 2, inter, factors, [total], [(theirs, tuple(range(WIN // 2 + 1))), (diagonal, one)], 1)
    late_first = len(near) + 2 + WIN // 2 + 2
    if aux_count == 1:
        residual, updated = block_sum(late_first, inter, factors, [total], late, ending=(scale, masked))
        return residual[None], updated[None]

    partial_sum = block_sum(late_first, inter, factors, [total], late)[None]
    pno_width = amplitudes.shape[1]
    row_span = pno_width // aux_count
    first_row = lax.axis_index("aux") * row_span
    live_rows = jnp.arange(pno_width)[None, :] < ranks[:, None]
    square_mask = live_rows[:, :, None] & live_rows[:, None, :]
    summed = lax.psum_scatter(partial_sum, "aux", scatter_dimension=1, tiled=True)
    row_energy = lax.dynamic_slice_in_dim(energies, first_row, row_span, 1)
    denominator = row_energy[:, :, None] + energies[:, None, :]
    row_amp = lax.dynamic_slice_in_dim(masked[None], first_row, row_span, 1).astype(F32)
    row_mask = lax.dynamic_slice_in_dim(square_mask, first_row, row_span, 1)
    residual = jnp.where(row_mask, summed + denominator * row_amp, jnp.zeros((), F32))
    return (residual, row_amp - residual / denominator)


def solution(mesh):
    return jax.shard_map(
        shards,
        mesh=mesh,
        in_specs=(
            P("pair", None, None),
            P("pair"),
            P("pair", "aux"),
            P("pair", "aux", None, None),
            P("pair", "aux"),
            P("pair", None),
            P("pair", None, "aux", None),
        ),
        out_specs=(P("pair", "aux", None), P("pair", "aux", None)),
        check_vma=False,
    )
```
